1024 devices in a mesh: dp: 16 (over z, x_lo), mp: 64 (over y, x_hi, core).
Axes of the slice: x: 8 (x_hi: 4, x_lo: 2; x = x_hi * 2 + x_lo), y: 8, z: 8, core: 2. Of those that a mesh axis runs over, the one named last changes fastest.
Arguments:
- grad_parts: bfloat16 [16, 32, 1024, 1024], P('dp', None, 'mp'), may hold values from -5 to 5
- momentum: float32 [32, 1024, 1024], P('dp', 'mp'), may hold values from -3 to 3
- second_moment: float32 [32, 1024, 1024], P('dp', 'mp'), may hold values from 0.02 to 0.5
- left_basis: bfloat16 [32, 1024, 1024], P('dp'), may hold values from -1 to 2
- right_basis: bfloat16 [32, 1024, 1024], P('dp'), may hold values from -1 to 2
- lr_scale: float32 [32], P('dp'), may hold values from 0.25 to 1
Outputs:
- update: float32 [32, 1024, 1024], P('dp', 'mp')
- momentum_out: float32 [32, 1024, 1024], P('dp', 'mp')
- second_out: float32 [32, 1024, 1024], P('dp', 'mp')
The draws below stay inside these ranges and needn't reach their ends.
All inputs are finite; a program needn't handle non-finite values.
Results may differ from the reference program's by a relative error of at most 0.023.
Values may be sent and summed in bfloat16 or wider, within the bound.
No kernel may reach another device: no remote copies, remote signals or barrier semaphores. Data moves between devices by JAX's collectives and lax.ppermute only.
A program may use at most 32 MiB of HBM per device.

```python
import math
import jax
import jax.numpy as jnp
from jax import lax

BLOCK = 1024
NBLK = 32
REPL = 16


def shape_basis(key, offdiag):
    size = (NBLK, BLOCK, BLOCK)
    rows = lax.broadcasted_iota(jnp.int32, size, 1)
    cols = lax.broadcasted_iota(jnp.int32, size, 2)
    diagonal = jax.random.uniform(key, size, jnp.float32, 0.8, 1.2)
    values = jnp.where(rows == cols, diagonal, offdiag * (0.35 / math.sqrt(BLOCK)))
    return values.astype(jnp.bfloat16)


def draw_left_basis(key, part):
    key = jax.random.fold_in(key, 11)
    key_diag, key_off = jax.random.split(key)
    size = (NBLK, BLOCK, BLOCK)
    offdiag = jnp.clip(jax.random.normal(key_off, size, jnp.float32), -6.0, 6.0)
    return shape_basis(key_diag, offdiag)


def draw_right_basis(key, part):
    key = jax.random.fold_in(key, 23)
    key_diag, key_off = jax.random.split(key)
    size = (NBLK, BLOCK, BLOCK)
    offdiag = jnp.clip(jax.random.normal(key_off, size, jnp.float32), -6.0, 6.0)
    return shape_basis(key_diag, offdiag)


def strengthened(entries, stream_key, source, target, shards_of, factor):
    owner, partner = [(jnp.arange(entries.shape[dim]) // (entries.shape[dim] // shards_of)).reshape([-1 if axis == dim else 1 for axis in range(entries.ndim)]) for dim in (source, target)]
    chosen = jax.random.permutation(stream_key, shards_of)[partner]
    strong = (owner == chosen) | (owner == (partner + shards_of // 2) % shards_of)
    return jnp.where(strong, factor * entries, entries)


def levels(own_key, dims, shards, smallest, high):
    level, own = 1.0, jax.random.fold_in(own_key, 6)
    for dim, blocks in shards:
        steps = jnp.exp(jax.random.uniform(jax.random.fold_in(own, dim), (blocks,), jnp.float32, smallest / len(shards), high / len(shards)))
        level = level * jnp.repeat(steps, dims[dim] // blocks).reshape([-1 if axis == dim else 1 for axis in range(len(dims))])
    return level


def noise(stream_key, shape, deviation, reach, shards=(), dtype=jnp.bfloat16):
    level = levels(stream_key, shape, shards, -0.22, 0.18) if shards else 1.0
    values = jax.random.normal(stream_key, shape, jnp.float32) * deviation * level
    return jnp.minimum(jnp.maximum(values, -reach), reach).astype(dtype)


def bell_draw_with(key, extent, scale, limit, shards, heavy, kind=jnp.bfloat16):
    drawn = scale * jax.random.normal(key, extent, jnp.float32)
    if shards:
        drawn = drawn * levels(key, extent, shards, -0.22, 0.18)
    return jnp.clip(strengthened(drawn, jax.random.fold_in(key, 3), *heavy), -limit, limit).astype(kind)


def setup_inputs(seed: int = 0) -> dict:
    arg_keys = jax.random.split(jax.random.key(seed), 7)
    return {
        "grad_parts": bell_draw_with(arg_keys[0], (REPL, NBLK, BLOCK, BLOCK), 0.25, 5.0, ((0, 16), (2, 64)), (0, 1, 16, 2.0)),
        "momentum": noise(arg_keys[1], (NBLK, BLOCK, BLOCK), 0.2, 3.0, ((0, 16), (1, 64)), jnp.float32),
        "second_moment": jnp.clip(jnp.exp(math.log(0.5) - 3.218876 * jax.random.uniform(arg_keys[2], (NBLK, BLOCK, BLOCK), jnp.float32) ** levels(arg_keys[2], (NBLK, BLOCK, BLOCK), ((0, 16), (1, 64)), -0.2, 0.2)), 0.02, 0.5),
        "left_basis": draw_left_basis(jax.random.fold_in(arg_keys[6], 71), 0),
        "right_basis": draw_right_basis(jax.random.fold_in(arg_keys[6], 71), 0),
        "lr_scale": jnp.clip(jnp.exp(math.log(1.0) - 1.3862944 * jax.random.uniform(arg_keys[5], (NBLK,), jnp.float32) ** levels(arg_keys[5], (NBLK,), ((0, 16),), -0.2, 0.2)), 0.25, 1.0),
    }


beta_one = 0.95
beta_two = 0.95
epsilon = 1e-08
bias_one = 1.0 - 0.95 ** 10
bias_two = 1.0 - 0.95 ** 10

def product(first, second):
    return jnp.dot(first.astype(jnp.float32), second.astype(jnp.float32), precision=lax.Precision.HIGHEST)

def handle(items):
    parts, moment, second, left, right, scale = items
    grad_sum = lax.optimization_barrier(jnp.sum(parts.astype(jnp.float32), axis=0))
    moment_new = beta_one * moment + (1.0 - beta_one) * grad_sum
    grad_half = grad_sum.astype(jnp.bfloat16)
    moment_half = moment_new.astype(jnp.bfloat16)
    turned_grad = product(grad_half, left).T.astype(jnp.bfloat16)
    turned_moment = product(moment_half, left).T.astype(jnp.bfloat16)
    rotated_grad = product(turned_grad, right)
    rotated_moment = product(turned_moment, right)
    second_new = beta_two * second + (1.0 - beta_two) * rotated_grad * rotated_grad
    ratio = (rotated_moment / bias_one / (jnp.sqrt(second_new / bias_two) + epsilon)).astype(jnp.bfloat16)
    returned = product(right, ratio.T).T.astype(jnp.bfloat16)
    full_step_t = product(returned.T, left.T)
    return (scale * full_step_t, moment_new, second_new)

def reference(grad_parts, momentum, second_moment, left_basis, right_basis, lr_scale):
    update, momentum_out, second_out = lax.map(handle, (jnp.swapaxes(grad_parts, 0, 1), momentum, second_moment, left_basis, right_basis, lr_scale))
    return (update, momentum_out, second_out)
```

```python
import jax
import jax.numpy as jnp
from jax import lax
from jax.sharding import Mesh, PartitionSpec as P

beta_one = 0.95
beta_two = 0.95
epsilon = 1e-08
bias_one = 1.0 - 0.95**10
bias_two = 1.0 - 0.95**10


MP = ("y", "xh", "c")
DP = ("z", "xl")


def turn_left(grad_sum, moment, left):
    moment_new = beta_one * moment + (1.0 - beta_one) * grad_sum
    stacked = jnp.stack([grad_sum.astype(jnp.bfloat16), moment_new.astype(jnp.bfloat16)], axis=1)
    turned = jnp.einsum("bik,bxji->bxkj", left, stacked, preferred_element_type=jnp.float32)
    return (turned.astype(jnp.bfloat16), moment_new)


def local(grad_parts, momentum, second_moment, left_basis, right_basis, lr_scale):
    parts = grad_parts[0].reshape(8, 2, 2, 16, 1024)
    side = lax.axis_index("xl")
    away = lax.dynamic_index_in_dim(parts, 1 - side, 1, keepdims=False)
    kept = lax.dynamic_index_in_dim(parts, side, 1, keepdims=False)
    came = lax.ppermute(away, "xl", [(0, 1), (1, 0)])
    pair = (kept.astype(jnp.float32) + came.astype(jnp.float32)).astype(jnp.bfloat16)
    shares = lax.all_to_all(pair, "z", split_axis=0, concat_axis=0, tiled=True)
    grad_sum = jnp.sum(shares.astype(jnp.float32), axis=0)
    turned, momentum_out = turn_left(grad_sum, momentum, left_basis)
    arrived = lax.all_to_all(turned, MP, split_axis=2, concat_axis=3, tiled=True)
    rotated = jnp.einsum("bxkj,bjl->bxkl", arrived, right_basis, preferred_element_type=jnp.float32)
    rotated_grad = rotated[:, 0]
    rotated_moment = rotated[:, 1]
    second_out = beta_two * second_moment + (1.0 - beta_two) * rotated_grad * rotated_grad
    ratio = (rotated_moment / bias_one / (jnp.sqrt(second_out / bias_two) + epsilon)).astype(
        jnp.bfloat16
    )
    returned = jnp.einsum(
        "bkl,bjl->bkj", ratio, right_basis, preferred_element_type=jnp.float32
    ).astype(jnp.bfloat16)
    landed = lax.all_to_all(returned, MP, split_axis=2, concat_axis=1, tiled=True)
    full_step = jnp.einsum("bik,bkj->bji", left_basis, landed, preferred_element_type=jnp.float32)
    update = lr_scale[:, None, None] * full_step
    return (update, momentum_out, second_out)


def solution(mesh):
    fine = Mesh(mesh.devices.reshape(8, 2, 8, 4, 2), DP + MP)
    in_specs = (
        P(DP, None, MP, None),
        P(DP, MP, None),
        P(DP, MP, None),
        P(DP, None, None),
        P(DP, None, None),
        P(DP),
    )
    out_specs = (P(DP, MP, None), P(DP, MP, None), P(DP, MP, None))
    return jax.shard_map(local, mesh=fine, in_specs=in_specs, out_specs=out_specs, check_vma=False)
```

```python
import jax
import jax.numpy as jnp
from jax import lax
from jax.experimental import pallas as pl
from jax.experimental.pallas import tpu as pltpu
from jax.sharding import Mesh, PartitionSpec as P

beta_one = 0.95
beta_two = 0.95
epsilon = 1e-08
bias_one = 1.0 - 0.95**10
bias_two = 1.0 - 0.95**10

MP = ("y", "xh", "c")
DP = ("z", "xl")
F32 = jnp.float32
BF16 = jnp.bfloat16
VMEM = pl.BlockSpec(memory_space=pltpu.VMEM)
SMEM = pl.BlockSpec(memory_space=pltpu.SMEM)
PARAMS = pltpu.CompilerParams(vmem_limit_bytes=24 * 1024 * 1024)


def swap_groups(pieces):
    lane = lax.broadcasted_iota(jnp.int32, (64, 128), 1)
    pieces = list(pieces)
    for bit in (1, 2, 4):
        low = (lane // (16 * bit)) % 2 == 0
        for first in range(8):
            if first & bit:
                continue
            a, b = pieces[first], pieces[first | bit]
            pieces[first] = jnp.where(low, a, pltpu.roll(b, 16 * bit, 1))
            pieces[first | bit] = jnp.where(low, pltpu.roll(a, 128 - 16 * bit, 1), b)
    return pieces


def lane_tiles_to_rows(eight):
    return jnp.concatenate([eight[:, 128 * t : 128 * t + 128] for t in range(8)], axis=0)


def to_messages(pieces):
    swapped = [piece.reshape(8, 8, 128) for piece in swap_groups(pieces)]
    return jnp.stack(swapped, axis=1).reshape(512, 128).astype(BF16)


def from_messages(arrived, shift):
    wide = arrived.astype(F32)
    later = pltpu.roll(wide, 128 - shift, 1)
    rows = jnp.stack([wide.reshape(64, 8, 128), later.reshape(64, 8, 128)], axis=1)
    return rows.reshape(1024, 128).T


def turn_kernel(shares, moment, left, moment_out, message):
    turned = []
    for b in range(2):
        grad = shares[0, b].astype(F32)
        for r in range(1, 8):
            grad = grad + shares[r, b].astype(F32)
        new = beta_one * moment[b] + (1.0 - beta_one) * grad
        moment_out[b] = new
        both = jnp.concatenate([grad.astype(BF16), new.astype(BF16)], axis=0)
        turned.append(jnp.dot(both, left[b], preferred_element_type=F32))
    pieces = [
        lane_tiles_to_rows(turned[b][16 * x + 8 * half : 16 * x + 8 * half + 8])
        for half in range(2)
        for b in range(2)
        for x in range(2)
    ]
    message[...] = to_messages(pieces)


def step_kernel(arrived, second, right, second_out, message):
    turned = from_messages(arrived[...], 64)[:64].astype(BF16)
    returned = []
    for b in range(2):
        rotated = jnp.dot(turned[32 * b : 32 * b + 32], right[b], preferred_element_type=F32)
        grad, moment = rotated[:16], rotated[16:]
        new = beta_two * second[b] + (1.0 - beta_two) * grad * grad
        second_out[b] = new
        ratio = (moment / bias_one / (jnp.sqrt(new / bias_two) + epsilon)).astype(BF16)
        returned.append(
            lax.dot_general(ratio, right[b], (((1,), (1,)), ((), ())), preferred_element_type=F32)
        )
    pieces = [
        lane_tiles_to_rows(returned[b][8 * half : 8 * half + 8])
        for half in range(2)
        for b in range(2)
    ]
    message[...] = to_messages(pieces + [jnp.zeros((64, 128), F32)] * 4)


def back_kernel(scale, arrived, left, update):
    returned = from_messages(arrived[...], 32)[:32].astype(BF16)
    for b in range(2):
        step = lax.dot_general(
            returned[16 * b : 16 * b + 16],
            left[b],
            (((1,), (1,)), ((), ())),
            preferred_element_type=F32,
        )
        update[b] = scale[b] * step


def strips():
    return jax.ShapeDtypeStruct((2, 16, 1024), F32)


def messages():
    return jax.ShapeDtypeStruct((512, 128), BF16)


def cost(products, size):
    return pl.CostEstimate(flops=2 * products * 1024 * 1024, bytes_accessed=size, transcendentals=0)


def turn(shares, momentum, left):
    return pl.pallas_call(
        turn_kernel,
        out_shape=(strips(), messages()),
        in_specs=[VMEM] * 3,
        out_specs=(VMEM, VMEM),
        compiler_params=PARAMS,
        cost_estimate=cost(64, 5 << 20),
        name="turn",
    )(shares, momentum, left)


def step(arrived, second, right):
    return pl.pallas_call(
        step_kernel,
        out_shape=(strips(), messages()),
        in_specs=[VMEM] * 3,
        out_specs=(VMEM, VMEM),
        compiler_params=PARAMS,
        cost_estimate=cost(96, 5 << 20),
        name="step",
    )(arrived, second, right)


def back(scale, arrived, left):
    return pl.pallas_call(
        back_kernel,
        out_shape=strips(),
        in_specs=[SMEM, VMEM, VMEM],
        out_specs=VMEM,
        compiler_params=PARAMS,
        cost_estimate=cost(32, 5 << 20),
        name="back",
    )(scale, arrived, left)


def trade(message):
    return lax.all_to_all(message, MP, split_axis=0, concat_axis=0, tiled=True)


def local(grad_parts, momentum, second_moment, left_basis, right_basis, lr_scale):
    parts = grad_parts[0].reshape(8, 2, 2, 16, 1024)
    side = lax.axis_index("xl")
    away = lax.dynamic_index_in_dim(parts, 1 - side, 1, keepdims=False)
    kept = lax.dynamic_index_in_dim(parts, side, 1, keepdims=False)
    came = lax.ppermute(away, "xl", [(0, 1), (1, 0)])
    pair = (kept.astype(F32) + came.astype(F32)).astype(BF16)
    shares = lax.all_to_all(pair, "z", split_axis=0, concat_axis=0, tiled=True)
    momentum_out, message = turn(shares, momentum, left_basis)
    second_out, message = step(trade(message), second_moment, right_basis)
    update = back(lr_scale, trade(message), left_basis)
    return (update, momentum_out, second_out)


def solution(mesh):
    fine = Mesh(mesh.devices.reshape(8, 2, 8, 4, 2), DP + MP)
    in_specs = (
        P(DP, None, MP, None),
        P(DP, MP, None),
        P(DP, MP, None),
        P(DP, None, None),
        P(DP, None, None),
        P(DP),
    )
    out_specs = (P(DP, MP, None), P(DP, MP, None), P(DP, MP, None))
    return jax.shard_map(local, mesh=fine, in_specs=in_specs, out_specs=out_specs, check_vma=False)
```

```python
import jax
import jax.numpy as jnp
from jax import lax
from jax.experimental import pallas as pl
from jax.experimental.pallas import tpu as pltpu
from jax.sharding import Mesh, PartitionSpec as P

beta_one = 0.95
beta_two = 0.95
epsilon = 1e-08
bias_one = 1.0 - 0.95**10
bias_two = 1.0 - 0.95**10

MP = ("y", "xh", "c")
DP = ("z", "xl")
F32 = jnp.float32
BF16 = jnp.bfloat16
VMEM = pl.BlockSpec(memory_space=pltpu.VMEM)
SMEM = pl.BlockSpec(memory_space=pltpu.SMEM)
PARAMS = pltpu.CompilerParams(vmem_limit_bytes=24 * 1024 * 1024)


def swap_groups(pieces):
    lane = lax.broadcasted_iota(jnp.int32, (64, 128), 1)
    pieces = list(pieces)
    for bit in (1, 2, 4):
        low = (lane // (16 * bit)) % 2 == 0
        for first in range(8):
            if first & bit:
                continue
            a, b = pieces[first], pieces[first | bit]
            pieces[first] = jnp.where(low, a, pltpu.roll(b, 16 * bit, 1))
            pieces[first | bit] = jnp.where(low, pltpu.roll(a, 128 - 16 * bit, 1), b)
    return pieces


def lane_tiles_to_rows(eight):
    return jnp.concatenate([eight[:, 128 * t : 128 * t + 128] for t in range(8)], axis=0)


def to_messages(pieces):
    swapped = [piece.reshape(8, 8, 128) for piece in swap_groups(pieces)]
    return jnp.stack(swapped, axis=1).reshape(512, 128).astype(BF16)


def from_messages(arrived, shift):
    wide = arrived.astype(F32)
    later = pltpu.roll(wide, 128 - shift, 1)
    rows = jnp.stack([wide.reshape(64, 8, 128), later.reshape(64, 8, 128)], axis=1)
    return rows.reshape(1024, 128).T


def turn_kernel(shares, moment, left, moment_out, message):
    turned = []
    for b in range(2):
        grad = shares[0, b].astype(F32)
        for r in range(1, 8):
            grad = grad + shares[r, b].astype(F32)
        new = beta_one * moment[b] + (1.0 - beta_one) * grad
        moment_out[b] = new
        both = jnp.concatenate([grad.astype(BF16), new.astype(BF16)], axis=0)
        turned.append(jnp.dot(both, left[b], preferred_element_type=F32))
    pieces = [
        lane_tiles_to_rows(turned[b][16 * x + 8 * half : 16 * x + 8 * half + 8])
        for half in range(2)
        for b in range(2)
        for x in range(2)
    ]
    message[...] = to_messages(pieces)


def step_kernel(arrived, second, right, second_out, message):
    turned = from_messages(arrived[...], 64)[:64].astype(BF16)
    returned = []
    for b in range(2):
        rotated = jnp.dot(turned[32 * b : 32 * b + 32], right[b], preferred_element_type=F32)
        grad, moment = rotated[:16], rotated[16:]
        new = beta_two * second[b] + (1.0 - beta_two) * grad * grad
        second_out[b] = new
        ratio = (moment / bias_one / (jnp.sqrt(new / bias_two) + epsilon)).astype(BF16)
        returned.append(
            lax.dot_general(ratio, right[b], (((1,), (1,)), ((), ())), preferred_element_type=F32)
        )
    pieces = [
        lane_tiles_to_rows(returned[b][8 * half : 8 * half + 8])
        for half in range(2)
        for b in range(2)
    ]
    message[...] = to_messages(pieces + [jnp.zeros((64, 128), F32)] * 4)


def back_kernel(scale, arrived, left, update):
    returned = from_messages(arrived[...], 32)[:32].astype(BF16)
    for b in range(2):
        step = lax.dot_general(
            returned[16 * b : 16 * b + 16],
            left[b],
            (((1,), (1,)), ((), ())),
            preferred_element_type=F32,
        )
        update[b] = scale[b] * step


def away_kernel(side, parts, away, sem):
    copy = pltpu.make_async_copy(parts.at[:, 1 - side[0]], away, sem)
    copy.start()
    copy.wait()


def hold_kernel(side, parts, left, right, kept, left_held, right_held, sems):
    copies = [
        pltpu.make_async_copy(parts.at[:, side[0]], kept, sems.at[0]),
        pltpu.make_async_copy(left, left_held, sems.at[1]),
        pltpu.make_async_copy(right, right_held, sems.at[2]),
    ]
    for copy in copies:
        copy.start()
    for copy in copies:
        copy.wait()


def strips():
    return jax.ShapeDtypeStruct((2, 16, 1024), F32)


def messages():
    return jax.ShapeDtypeStruct((512, 128), BF16)


def cost(products, size):
    return pl.CostEstimate(flops=2 * products * 1024 * 1024, bytes_accessed=size, transcendentals=0)


ANY = pl.BlockSpec(memory_space=pl.ANY)


def half():
    return jax.ShapeDtypeStruct((8, 2, 16, 1024), BF16)


def take_away(side, parts):
    return pl.pallas_call(
        away_kernel,
        out_shape=half(),
        in_specs=[SMEM, ANY],
        out_specs=ANY,
        scratch_shapes=[pltpu.SemaphoreType.DMA],
        compiler_params=PARAMS,
        cost_estimate=cost(0, 1 << 20),
        name="take_away",
    )(side, parts)


def hold(side, parts, left, right):
    basis = jax.ShapeDtypeStruct((2, 1024, 1024), BF16)
    return pl.pallas_call(
        hold_kernel,
        out_shape=(half(), basis, basis),
        in_specs=[SMEM, ANY, ANY, ANY],
        out_specs=(ANY, ANY, ANY),
        scratch_shapes=[pltpu.SemaphoreType.DMA((3,))],
        compiler_params=PARAMS,
        cost_estimate=cost(0, 18 << 20),
        name="hold",
    )(side, parts, left, right)


def turn(shares, momentum, left):
    return pl.pallas_call(
        turn_kernel,
        out_shape=(strips(), messages()),
        in_specs=[VMEM] * 3,
        out_specs=(VMEM, VMEM),
        compiler_params=PARAMS,
        cost_estimate=cost(64, 5 << 20),
        name="turn",
    )(shares, momentum, left)


def step(arrived, second, right):
    return pl.pallas_call(
        step_kernel,
        out_shape=(strips(), messages()),
        in_specs=[VMEM] * 3,
        out_specs=(VMEM, VMEM),
        compiler_params=PARAMS,
        cost_estimate=cost(96, 5 << 20),
        name="step",
    )(arrived, second, right)


def back(scale, arrived, left):
    return pl.pallas_call(
        back_kernel,
        out_shape=strips(),
        in_specs=[SMEM, VMEM, VMEM],
        out_specs=VMEM,
        compiler_params=PARAMS,
        cost_estimate=cost(32, 5 << 20),
        name="back",
    )(scale, arrived, left)


def trade(message):
    return lax.all_to_all(message, MP, split_axis=0, concat_axis=0, tiled=True)


def local(grad_parts, momentum, second_moment, left_basis, right_basis, lr_scale):
    parts = grad_parts[0].reshape(8, 2, 2, 16, 1024)
    side = lax.axis_index("xl").reshape(1)
    away = take_away(side, parts)
    came = lax.ppermute(away, "xl", [(0, 1), (1, 0)])
    kept, left_basis, right_basis = hold(side, parts, left_basis, right_basis)
    pair = (kept.astype(F32) + came.astype(F32)).astype(BF16)
    shares = lax.all_to_all(pair, "z", split_axis=0, concat_axis=0, tiled=True)
    momentum_out, message = turn(shares, momentum, left_basis)
    second_out, message = step(trade(message), second_moment, right_basis)
    update = back(lr_scale, trade(message), left_basis)
    return (update, momentum_out, second_out)


def solution(mesh):
    fine = Mesh(mesh.devices.reshape(8, 2, 8, 4, 2), DP + MP)
    in_specs = (
        P(DP, None, MP, None),
        P(DP, MP, None),
        P(DP, MP, None),
        P(DP, None, None),
        P(DP, None, None),
        P(DP),
    )
    out_specs = (P(DP, MP, None), P(DP, MP, None), P(DP, MP, None))
    return jax.shard_map(local, mesh=fine, in_specs=in_specs, out_specs=out_specs, check_vma=False)
```

```python
import jax
import jax.numpy as jnp
from jax import lax
from jax.experimental import pallas as pl
from jax.experimental.pallas import tpu as pltpu
from jax.sharding import Mesh, PartitionSpec as P

beta_one = 0.95
beta_two = 0.95
epsilon = 1e-08
bias_one = 1.0 - 0.95**10
bias_two = 1.0 - 0.95**10

MP = ("y", "xh", "c")
DP = ("z", "xl")
F32 = jnp.float32
BF16 = jnp.bfloat16
VMEM = pl.BlockSpec(memory_space=pltpu.VMEM)
SMEM = pl.BlockSpec(memory_space=pltpu.SMEM)
PARAMS = pltpu.CompilerParams(vmem_limit_bytes=24 * 1024 * 1024)


def swap_groups(pieces):
    lane = lax.broadcasted_iota(jnp.int32, (64, 128), 1)
    pieces = list(pieces)
    for bit in (1, 2, 4):
        low = (lane // (16 * bit)) % 2 == 0
        for first in range(8):
            if first & bit:
                continue
            a, b = pieces[first], pieces[first | bit]
            pieces[first] = jnp.where(low, a, pltpu.roll(b, 16 * bit, 1))
            pieces[first | bit] = jnp.where(low, pltpu.roll(a, 128 - 16 * bit, 1), b)
    return pieces


def lane_tiles_to_rows(eight):
    return jnp.concatenate([eight[:, 128 * t : 128 * t + 128] for t in range(8)], axis=0)


def to_messages(pieces):
    swapped = [piece.reshape(8, 8, 128) for piece in swap_groups(pieces)]
    return jnp.stack(swapped, axis=1).reshape(512, 128).astype(BF16)


def from_messages(arrived, shift):
    wide = arrived.astype(F32)
    later = pltpu.roll(wide, 128 - shift, 1)
    rows = jnp.stack([wide.reshape(64, 8, 128), later.reshape(64, 8, 128)], axis=1)
    return rows.reshape(1024, 128).T


def turn_kernel(shares, moment, left, moment_out, message):
    turned = []
    for b in range(2):
        grad = shares[0, b].astype(F32)
        for r in range(1, 8):
            grad = grad + shares[r, b].astype(F32)
        new = beta_one * moment[b] + (1.0 - beta_one) * grad
        moment_out[b] = new
        both = jnp.concatenate([grad.astype(BF16), new.astype(BF16)], axis=0)
        turned.append(jnp.dot(both, left[b], preferred_element_type=F32))
    pieces = [
        lane_tiles_to_rows(turned[b][16 * x + 8 * half : 16 * x + 8 * half + 8])
        for half in range(2)
        for b in range(2)
        for x in range(2)
    ]
    message[...] = to_messages(pieces)


def step_kernel(arrived, second, right, right_turned, second_out, message):
    turned = from_messages(arrived[...], 64)[:64].astype(BF16)
    returned = []
    for b in range(2):
        rotated = jnp.dot(turned[32 * b : 32 * b + 32], right[b], preferred_element_type=F32)
        grad, moment = rotated[:16], rotated[16:]
        new = beta_two * second[b] + (1.0 - beta_two) * grad * grad
        second_out[b] = new
        ratio = (moment / bias_one / (jnp.sqrt(new / bias_two) + epsilon)).astype(BF16)
        returned.append(
            jnp.dot(ratio, right_turned[b], preferred_element_type=F32)
        )
    pieces = [
        lane_tiles_to_rows(returned[b][8 * half : 8 * half + 8])
        for half in range(2)
        for b in range(2)
    ]
    message[...] = to_messages(pieces + [jnp.zeros((64, 128), F32)] * 4)


def back_kernel(scale, arrived, left, update, fresh, sems):
    writes = []
    returned = from_messages(arrived[...], 32)[:32].astype(BF16)
    for b in range(2):
        step = jnp.dot(returned[16 * b : 16 * b + 16], left[b], preferred_element_type=F32)
        fresh[b] = scale[b][:, :1] * step
        writes.append(pltpu.make_async_copy(fresh.at[b], update.at[b], sems.at[b]))
        writes[b].start()
    for write in writes:
        write.wait()


def away_kernel(side, parts, away, sem):
    copy = pltpu.make_async_copy(parts.at[:, 1 - side[0]], away, sem)
    copy.start()
    copy.wait()


def hold_kernel(
    side, parts, left, right, kept, left_held, right_held, right_turned, left_turned, sems
):
    copies = [
        pltpu.make_async_copy(parts.at[:, side[0]], kept, sems.at[0]),
        pltpu.make_async_copy(left, left_held, sems.at[1]),
        pltpu.make_async_copy(right, right_held, sems.at[2]),
    ]
    for copy in copies:
        copy.start()
    for b in range(2):
        left_turned[b] = left[b].T
        right_turned[b] = right[b].T
    for copy in copies:
        copy.wait()


def strips():
    return jax.ShapeDtypeStruct((2, 16, 1024), F32)


def messages():
    return jax.ShapeDtypeStruct((512, 128), BF16)


def cost(products, size):
    return pl.CostEstimate(flops=2 * products * 1024 * 1024, bytes_accessed=size, transcendentals=0)


FRESH = [pltpu.VMEM((2, 16, 1024), F32), pltpu.SemaphoreType.DMA((2,))]
HBM = pl.BlockSpec(memory_space=pltpu.HBM)
ANY = pl.BlockSpec(memory_space=pl.ANY)


def half():
    return jax.ShapeDtypeStruct((8, 2, 16, 1024), BF16)


def take_away(side, parts):
    return pl.pallas_call(
        away_kernel,
        out_shape=half(),
        in_specs=[SMEM, HBM],
        out_specs=ANY,
        scratch_shapes=[pltpu.SemaphoreType.DMA],
        compiler_params=PARAMS,
        cost_estimate=cost(0, 1 << 20),
        name="take_away",
    )(side, parts)


def hold(side, parts, left, right):
    basis = jax.ShapeDtypeStruct((2, 1024, 1024), BF16)
    return pl.pallas_call(
        hold_kernel,
        out_shape=(half(), basis, basis, basis, basis),
        in_specs=[SMEM, HBM, VMEM, VMEM],
        out_specs=(ANY, ANY, ANY, VMEM, VMEM),
        scratch_shapes=[pltpu.SemaphoreType.DMA((3,))],
        compiler_params=PARAMS,
        cost_estimate=cost(0, 18 << 20),
        name="hold",
    )(side, parts, left, right)


def turn(shares, momentum, left):
    return pl.pallas_call(
        turn_kernel,
        out_shape=(strips(), messages()),
        in_specs=[VMEM] * 3,
        out_specs=(VMEM, VMEM),
        compiler_params=PARAMS,
        cost_estimate=cost(64, 5 << 20),
        name="turn",
    )(shares, momentum, left)


def step(arrived, second, right, right_turned):
    return pl.pallas_call(
        step_kernel,
        out_shape=(strips(), messages()),
        in_specs=[VMEM] * 4,
        out_specs=(VMEM, VMEM),
        compiler_params=PARAMS,
        cost_estimate=cost(96, 5 << 20),
        name="step",
    )(arrived, second, right, right_turned)


def back(scale, arrived, left):
    return pl.pallas_call(
        back_kernel,
        out_shape=strips(),
        in_specs=[VMEM, VMEM, VMEM],
        out_specs=ANY,
        scratch_shapes=FRESH,
        compiler_params=PARAMS,
        cost_estimate=cost(32, 5 << 20),
        name="back",
    )(scale, arrived, left)


def spread(scale):
    return jnp.broadcast_to(scale[:, None, None], (2, 16, 128))


def trade(message):
    return lax.all_to_all(message, MP, split_axis=0, concat_axis=0, tiled=True)


def local(grad_parts, momentum, second_moment, left_basis, right_basis, lr_scale):
    parts = grad_parts[0].reshape(8, 2, 2, 16, 1024)
    side = lax.axis_index("xl").reshape(1)
    away = take_away(side, parts)
    came = lax.ppermute(away, "xl", [(0, 1), (1, 0)])
    kept, left, right, right_turned, left_turned = hold(side, parts, left_basis, right_basis)
    pair = (kept.astype(F32) + came.astype(F32)).astype(BF16)
    shares = lax.all_to_all(pair, "z", split_axis=0, concat_axis=0, tiled=True)
    momentum_out, message = turn(shares, momentum, left)
    second_out, message = step(trade(message), second_moment, right, right_turned)
    update = back(spread(lr_scale), trade(message), left_turned)
    return (update, momentum_out, second_out)


def solution(mesh):
    fine = Mesh(mesh.devices.reshape(8, 2, 8, 4, 2), DP + MP)
    in_specs = (
        P(DP, None, MP, None),
        P(DP, MP, None),
        P(DP, MP, None),
        P(DP, None, None),
        P(DP, None, None),
        P(DP),
    )
    out_specs = (P(DP, MP, None), P(DP, MP, None), P(DP, MP, None))
    return jax.shard_map(local, mesh=fine, in_specs=in_specs, out_specs=out_specs, check_vma=False)
```

```python
import jax
import jax.numpy as jnp
from jax import lax
from jax.experimental import pallas as pl
from jax.experimental.pallas import tpu as pltpu
from jax.sharding import Mesh, PartitionSpec as P

beta_one = 0.95
beta_two = 0.95
epsilon = 1e-08
bias_one = 1.0 - 0.95**10
bias_two = 1.0 - 0.95**10

MP = ("y", "xh", "c")
DP = ("z", "xl")
F32 = jnp.float32
BF16 = jnp.bfloat16
VMEM = pl.BlockSpec(memory_space=pltpu.VMEM)
SMEM = pl.BlockSpec(memory_space=pltpu.SMEM)
PARAMS = pltpu.CompilerParams(vmem_limit_bytes=24 * 1024 * 1024)


def swap_groups(pieces):
    lane = lax.broadcasted_iota(jnp.int32, (64, 128), 1)
    pieces = list(pieces)
    for bit in (1, 2, 4):
        low = (lane // (16 * bit)) % 2 == 0
        for first in range(8):
            if first & bit:
                continue
            a, b = pieces[first], pieces[first | bit]
            pieces[first] = jnp.where(low, a, pltpu.roll(b, 16 * bit, 1))
            pieces[first | bit] = jnp.where(low, pltpu.roll(a, 128 - 16 * bit, 1), b)
    return pieces


def lane_tiles_to_rows(eight):
    return jnp.concatenate([eight[:, 128 * t : 128 * t + 128] for t in range(8)], axis=0)


def to_messages(pieces):
    swapped = [piece.reshape(8, 8, 128) for piece in swap_groups(pieces)]
    return jnp.stack(swapped, axis=1).reshape(512, 128).astype(BF16)


def from_messages(arrived, shift):
    wide = arrived.astype(F32)
    later = pltpu.roll(wide, 128 - shift, 1)
    rows = jnp.stack([wide.reshape(64, 8, 128), later.reshape(64, 8, 128)], axis=1)
    return rows.reshape(1024, 128).T


def turn_kernel(shares, moment, left, moment_new, message):
    rows = []
    for b in range(2):
        grad = shares[0, b].astype(F32)
        for r in range(1, 8):
            grad = grad + shares[r, b].astype(F32)
        new = beta_one * moment[b] + (1.0 - beta_one) * grad
        moment_new[b] = new
        rows.append(jnp.concatenate([grad.astype(BF16), new.astype(BF16)], axis=0))
    turned = [jnp.dot(rows[b], left[b], preferred_element_type=F32) for b in range(2)]
    pieces = [
        lane_tiles_to_rows(turned[b][16 * x + 8 * half : 16 * x + 8 * half + 8])
        for half in range(2)
        for b in range(2)
        for x in range(2)
    ]
    message[...] = to_messages(pieces)


def step_kernel(arrived, second, right, right_turned, second_new, message):
    turned = from_messages(arrived[...], 64)[:64].astype(BF16)
    ratios = []
    for b in range(2):
        rotated = jnp.dot(turned[32 * b : 32 * b + 32], right[b], preferred_element_type=F32)
        grad, moment = rotated[:16], rotated[16:]
        new = beta_two * second[b] + (1.0 - beta_two) * grad * grad
        second_new[b] = new
        ratio = (moment / bias_one / (jnp.sqrt(new / bias_two) + epsilon)).astype(BF16)
        ratios.append(ratio)
    returned = [jnp.dot(ratios[b], right_turned[b], preferred_element_type=F32) for b in range(2)]
    pieces = [
        lane_tiles_to_rows(returned[b][8 * half : 8 * half + 8])
        for half in range(2)
        for b in range(2)
    ]
    message[...] = to_messages(pieces + [jnp.zeros((64, 128), F32)] * 4)


def back_kernel(
    scale, arrived, left, moment_new, second_new, update, moment_out, second_out, fresh, sems
):
    writes = [
        pltpu.make_async_copy(moment_new, moment_out, sems.at[2]),
        pltpu.make_async_copy(second_new, second_out, sems.at[3]),
    ]
    for write in writes:
        write.start()
    returned = from_messages(arrived[...], 32)[:32].astype(BF16)
    for b in range(2):
        step = jnp.dot(returned[16 * b : 16 * b + 16], left[b], preferred_element_type=F32)
        fresh[b] = scale[b][:, :1] * step
        writes.append(pltpu.make_async_copy(fresh.at[b], update.at[b], sems.at[b]))
        writes[-1].start()
    for write in writes:
        write.wait()


def away_kernel(side, parts, away, sem):
    copy = pltpu.make_async_copy(parts.at[:, 1 - side[0]], away, sem)
    copy.start()
    copy.wait()


def hold_kernel(
    side,
    scale,
    parts,
    left,
    right,
    kept,
    left_held,
    right_held,
    right_turned,
    left_turned,
    scale_rows,
    sems,
):
    copies = [
        pltpu.make_async_copy(parts.at[:, side[0]], kept, sems.at[0]),
        pltpu.make_async_copy(left, left_held, sems.at[1]),
        pltpu.make_async_copy(right, right_held, sems.at[2]),
    ]
    for copy in copies:
        copy.start()
    for b in range(2):
        scale_rows[b] = jnp.full((16, 128), scale[b], F32)
        left_turned[b] = left[b].T
        right_turned[b] = right[b].T
    for copy in copies:
        copy.wait()


def strips():
    return jax.ShapeDtypeStruct((2, 16, 1024), F32)


def messages():
    return jax.ShapeDtypeStruct((512, 128), BF16)


def cost(products, size):
    return pl.CostEstimate(flops=2 * products * 1024 * 1024, bytes_accessed=size, transcendentals=0)


FRESH = [pltpu.VMEM((2, 16, 1024), F32), pltpu.SemaphoreType.DMA((4,))]
HBM = pl.BlockSpec(memory_space=pltpu.HBM)
ANY = pl.BlockSpec(memory_space=pl.ANY)


def half():
    return jax.ShapeDtypeStruct((8, 2, 16, 1024), BF16)


def take_away(side, parts):
    return pl.pallas_call(
        away_kernel,
        out_shape=half(),
        in_specs=[SMEM, HBM],
        out_specs=ANY,
        scratch_shapes=[pltpu.SemaphoreType.DMA],
        compiler_params=PARAMS,
        cost_estimate=cost(0, 1 << 20),
        name="take_away",
    )(side, parts)


def hold(side, scale, parts, left, right):
    basis = jax.ShapeDtypeStruct((2, 1024, 1024), BF16)
    return pl.pallas_call(
        hold_kernel,
        out_shape=(half(), basis, basis, basis, basis, jax.ShapeDtypeStruct((2, 16, 128), F32)),
        in_specs=[SMEM, SMEM, HBM, VMEM, VMEM],
        out_specs=(ANY, ANY, ANY, VMEM, VMEM, VMEM),
        scratch_shapes=[pltpu.SemaphoreType.DMA((3,))],
        compiler_params=PARAMS,
        cost_estimate=cost(0, 18 << 20),
        name="hold",
    )(side, scale, parts, left, right)


def turn(shares, momentum, left):
    return pl.pallas_call(
        turn_kernel,
        out_shape=(strips(), messages()),
        in_specs=[VMEM] * 3,
        out_specs=(VMEM, VMEM),
        compiler_params=PARAMS,
        cost_estimate=cost(64, 5 << 20),
        name="turn",
    )(shares, momentum, left)


def step(arrived, second, right, right_turned):
    return pl.pallas_call(
        step_kernel,
        out_shape=(strips(), messages()),
        in_specs=[VMEM] * 4,
        out_specs=(VMEM, VMEM),
        compiler_params=PARAMS,
        cost_estimate=cost(96, 5 << 20),
        name="step",
    )(arrived, second, right, right_turned)


def back(scale, arrived, left, moment_new, second_new):
    return pl.pallas_call(
        back_kernel,
        out_shape=(strips(), strips(), strips()),
        in_specs=[VMEM] * 5,
        out_specs=(ANY, ANY, ANY),
        scratch_shapes=FRESH,
        compiler_params=PARAMS,
        cost_estimate=cost(32, 5 << 20),
        name="back",
    )(scale, arrived, left, moment_new, second_new)


def trade(message):
    return lax.all_to_all(message, MP, split_axis=0, concat_axis=0, tiled=True)


def local(grad_parts, momentum, second_moment, left_basis, right_basis, lr_scale):
    parts = grad_parts[0].reshape(8, 2, 2, 16, 1024)
    side = lax.axis_index("xl").reshape(1)
    away = take_away(side, parts)
    came = lax.ppermute(away, "xl", [(0, 1), (1, 0)])
    kept, left, right, right_turned, left_turned, scale_rows = hold(
        side, lr_scale, parts, left_basis, right_basis
    )
    pair = (kept.astype(F32) + came.astype(F32)).astype(BF16)
    shares = lax.all_to_all(pair, "z", split_axis=0, concat_axis=0, tiled=True)
    moment_new, message = turn(shares, momentum, left)
    second_new, message = step(trade(message), second_moment, right, right_turned)
    return back(scale_rows, trade(message), left_turned, moment_new, second_new)


def solution(mesh):
    fine = Mesh(mesh.devices.reshape(8, 2, 8, 4, 2), DP + MP)
    in_specs = (
        P(DP, None, MP, None),
        P(DP, MP, None),
        P(DP, MP, None),
        P(DP, None, None),
        P(DP, None, None),
        P(DP),
    )
    out_specs = (P(DP, MP, None), P(DP, MP, None), P(DP, MP, None))
    return jax.shard_map(local, mesh=fine, in_specs=in_specs, out_specs=out_specs, check_vma=False)
```

```python
import jax
import jax.numpy as jnp
from jax import lax
from jax.experimental import pallas as pl
from jax.experimental.pallas import tpu as pltpu
from jax.sharding import Mesh, PartitionSpec as P

beta_one = 0.95
beta_two = 0.95
epsilon = 1e-08
bias_one = 1.0 - 0.95**10
bias_two = 1.0 - 0.95**10

MP = ("y", "xh", "c")
DP = ("z", "xl")
F32 = jnp.float32
BF16 = jnp.bfloat16
VMEM = pl.BlockSpec(memory_space=pltpu.VMEM)
SMEM = pl.BlockSpec(memory_space=pltpu.SMEM)
PARAMS = pltpu.CompilerParams(vmem_limit_bytes=24 * 1024 * 1024)


def swap_groups(pieces):
    lane = lax.broadcasted_iota(jnp.int32, (64, 128), 1)
    pieces = list(pieces)
    for bit in (1, 2, 4):
        low = (lane // (16 * bit)) % 2 == 0
        for first in range(8):
            if first & bit:
                continue
            a, b = pieces[first], pieces[first | bit]
            pieces[first] = jnp.where(low, a, pltpu.roll(b, 16 * bit, 1))
            pieces[first | bit] = jnp.where(low, pltpu.roll(a, 128 - 16 * bit, 1), b)
    return pieces


def lane_tiles_to_rows(eight):
    return jnp.concatenate([eight[:, 128 * t : 128 * t + 128] for t in range(8)], axis=0)


def to_messages(pieces):
    swapped = [piece.reshape(8, 8, 128) for piece in swap_groups(pieces)]
    return jnp.stack(swapped, axis=1).reshape(512, 128).astype(BF16)


def from_messages(arrived, shift):
    wide = arrived.astype(F32)
    later = pltpu.roll(wide, 128 - shift, 1)
    rows = jnp.stack([wide.reshape(64, 8, 128), later.reshape(64, 8, 128)], axis=1)
    return rows.reshape(1024, 128).T


def turn_kernel(shares, moment, left, moment_new, message):
    rows = []
    for b in range(2):
        grad = shares[0, b].astype(F32)
        for r in range(1, 8):
            grad = grad + shares[r, b].astype(F32)
        new = beta_one * moment[b] + (1.0 - beta_one) * grad
        moment_new[b] = new
        rows.append(jnp.concatenate([grad.astype(BF16), new.astype(BF16)], axis=0))
    turned = [jnp.dot(rows[b], left[b], preferred_element_type=F32) for b in range(2)]
    pieces = [
        lane_tiles_to_rows(turned[b][16 * x + 8 * half : 16 * x + 8 * half + 8])
        for half in range(2)
        for b in range(2)
        for x in range(2)
    ]
    message[...] = to_messages(pieces)


def step_kernel(arrived, second, right, right_turned, second_new, message):
    turned = from_messages(arrived[...], 64)[:64].astype(BF16)
    ratios = []
    for b in range(2):
        rotated = jnp.dot(turned[32 * b : 32 * b + 32], right[b], preferred_element_type=F32)
        grad, moment = rotated[:16], rotated[16:]
        new = beta_two * second[b] + (1.0 - beta_two) * grad * grad
        second_new[b] = new
        ratio = (moment / bias_one / (jnp.sqrt(new / bias_two) + epsilon)).astype(BF16)
        ratios.append(ratio)
    returned = [jnp.dot(ratios[b], right_turned[b], preferred_element_type=F32) for b in range(2)]
    pieces = [
        lane_tiles_to_rows(returned[b][8 * half : 8 * half + 8])
        for half in range(2)
        for b in range(2)
    ]
    message[...] = to_messages(pieces + [jnp.zeros((64, 128), F32)] * 4)


def back_kernel(
    scale, arrived, left, moment_new, second_new, update, moment_out, second_out, fresh, sems
):
    writes = [
        pltpu.make_async_copy(moment_new, moment_out, sems.at[2]),
        pltpu.make_async_copy(second_new, second_out, sems.at[3]),
    ]
    for write in writes:
        write.start()
    returned = from_messages(arrived[...], 32)[:32].astype(BF16)
    for b in range(2):
        step = jnp.dot(returned[16 * b : 16 * b + 16], left[b], preferred_element_type=F32)
        fresh[b] = scale[b][:, :1] * step
        writes.append(pltpu.make_async_copy(fresh.at[b], update.at[b], sems.at[b]))
        writes[-1].start()
    for write in writes:
        write.wait()


def split_kernel(side, parts, first, last, kept, sems):
    copies = [
        pltpu.make_async_copy(parts.at[pl.ds(0, 4), 1 - side[0]], first, sems.at[0]),
        pltpu.make_async_copy(parts.at[pl.ds(4, 4), 1 - side[0]], last, sems.at[1]),
        pltpu.make_async_copy(parts.at[:, side[0]], kept, sems.at[2]),
    ]
    for copy in copies:
        copy.start()
    for copy in copies:
        copy.wait()


def hold_kernel(left, right, left_held, right_held, right_turned, left_turned, sems):
    copies = [
        pltpu.make_async_copy(left, left_held, sems.at[0]),
        pltpu.make_async_copy(right, right_held, sems.at[1]),
    ]
    for copy in copies:
        copy.start()
    for b in range(2):
        left_turned[b] = left[b].T
        right_turned[b] = right[b].T
    for copy in copies:
        copy.wait()


def strips():
    return jax.ShapeDtypeStruct((2, 16, 1024), F32)


def messages():
    return jax.ShapeDtypeStruct((512, 128), BF16)


def cost(products, size):
    return pl.CostEstimate(flops=2 * products * 1024 * 1024, bytes_accessed=size, transcendentals=0)


FRESH = [pltpu.VMEM((2, 16, 1024), F32), pltpu.SemaphoreType.DMA((4,))]
ANY = pl.BlockSpec(memory_space=pl.ANY)


def split(side, parts):
    quarter = jax.ShapeDtypeStruct((4, 2, 16, 1024), BF16)
    half = jax.ShapeDtypeStruct((8, 2, 16, 1024), BF16)
    return pl.pallas_call(
        split_kernel,
        out_shape=(quarter, quarter, half),
        in_specs=[SMEM, ANY],
        out_specs=(ANY, ANY, ANY),
        scratch_shapes=[pltpu.SemaphoreType.DMA((3,))],
        compiler_params=PARAMS,
        cost_estimate=cost(0, 2 << 20),
        name="split",
    )(side, parts)


def hold(left, right):
    basis = jax.ShapeDtypeStruct((2, 1024, 1024), BF16)
    return pl.pallas_call(
        hold_kernel,
        out_shape=(basis, basis, basis, basis),
        in_specs=[VMEM, VMEM],
        out_specs=(ANY, ANY, VMEM, VMEM),
        scratch_shapes=[pltpu.SemaphoreType.DMA((2,))],
        compiler_params=PARAMS,
        cost_estimate=cost(0, 24 << 20),
        name="hold",
    )(left, right)


def turn(shares, momentum, left):
    return pl.pallas_call(
        turn_kernel,
        out_shape=(strips(), messages()),
        in_specs=[VMEM] * 3,
        out_specs=(VMEM, VMEM),
        compiler_params=PARAMS,
        cost_estimate=cost(64, 5 << 20),
        name="turn",
    )(shares, momentum, left)


def step(arrived, second, right, right_turned):
    return pl.pallas_call(
        step_kernel,
        out_shape=(strips(), messages()),
        in_specs=[VMEM] * 4,
        out_specs=(VMEM, VMEM),
        compiler_params=PARAMS,
        cost_estimate=cost(96, 5 << 20),
        name="step",
    )(arrived, second, right, right_turned)


def back(scale, arrived, left, moment_new, second_new):
    return pl.pallas_call(
        back_kernel,
        out_shape=(strips(), strips(), strips()),
        in_specs=[VMEM] * 5,
        out_specs=(ANY, ANY, ANY),
        scratch_shapes=FRESH,
        compiler_params=PARAMS,
        cost_estimate=cost(32, 5 << 20),
        name="back",
    )(scale, arrived, left, moment_new, second_new)


def trade(message):
    return lax.all_to_all(message, MP, split_axis=0, concat_axis=0, tiled=True)


def local(grad_parts, momentum, second_moment, left_basis, right_basis, lr_scale):
    parts = grad_parts[0].reshape(8, 2, 2, 16, 1024)
    side = lax.axis_index("xl").reshape(1)
    *away, kept = split(side, parts)
    came = [lax.ppermute(piece, "xl", [(0, 1), (1, 0)]) for piece in away]
    left, right, right_turned, left_turned = hold(left_basis, right_basis)
    pair = (kept.astype(F32) + jnp.concatenate(came).astype(F32)).astype(BF16)
    shares = lax.all_to_all(pair, "z", split_axis=0, concat_axis=0, tiled=True)
    scale_rows = jnp.broadcast_to(lr_scale[:, None, None], (2, 16, 128))
    moment_new, message = turn(shares, momentum, left)
    second_new, message = step(trade(message), second_moment, right, right_turned)
    return back(scale_rows, trade(message), left_turned, moment_new, second_new)


def solution(mesh):
    fine = Mesh(mesh.devices.reshape(8, 2, 8, 4, 2), DP + MP)
    in_specs = (
        P(DP, None, MP, None),
        P(DP, MP, None),
        P(DP, MP, None),
        P(DP, None, None),
        P(DP, None, None),
        P(DP),
    )
    out_specs = (P(DP, MP, None), P(DP, MP, None), P(DP, MP, None))
    return jax.shard_map(local, mesh=fine, in_specs=in_specs, out_specs=out_specs, check_vma=False)
```

```python
import jax
import jax.numpy as jnp
from jax import lax
from jax.experimental import pallas as pl
from jax.experimental.pallas import tpu as pltpu
from jax.sharding import Mesh, PartitionSpec as P

beta_one = 0.95
beta_two = 0.95
epsilon = 1e-08
bias_one = 1.0 - 0.95**10
bias_two = 1.0 - 0.95**10

MP = ("y", "xh", "c")
DP = ("zh", "zl", "xl")
NEAR = ("zl", "xl", "c")
GROUP = DP + ("c",)
F32 = jnp.float32
BF16 = jnp.bfloat16
VMEM = pl.BlockSpec(memory_space=pltpu.VMEM)
SMEM = pl.BlockSpec(memory_space=pltpu.SMEM)
PARAMS = pltpu.CompilerParams(vmem_limit_bytes=24 * 1024 * 1024)


def swap_groups(pieces):
    lane = lax.broadcasted_iota(jnp.int32, (64, 128), 1)
    pieces = list(pieces)
    for bit in (1, 2, 4):
        low = (lane // (16 * bit)) % 2 == 0
        for first in range(8):
            if first & bit:
                continue
            a, b = pieces[first], pieces[first | bit]
            pieces[first] = jnp.where(low, a, pltpu.roll(b, 16 * bit, 1))
            pieces[first | bit] = jnp.where(low, pltpu.roll(a, 128 - 16 * bit, 1), b)
    return pieces


def lane_tiles_to_rows(eight):
    return jnp.concatenate([eight[:, 128 * t : 128 * t + 128] for t in range(8)], axis=0)


def to_messages(pieces):
    swapped = [piece.reshape(8, 8, 128) for piece in swap_groups(pieces)]
    return jnp.stack(swapped, axis=1).reshape(512, 128).astype(BF16)


def from_messages(arrived, shift):
    wide = arrived.astype(F32)
    later = pltpu.roll(wide, 128 - shift, 1)
    rows = jnp.stack([wide.reshape(64, 8, 128), later.reshape(64, 8, 128)], axis=1)
    return rows.reshape(1024, 128).T


def turn_kernel(shares, moment, left, moment_new, message):
    rows = []
    for b in range(2):
        grad = shares[0, b].astype(F32)
        for r in range(1, 8):
            grad = grad + shares[r, b].astype(F32)
        new = beta_one * moment[b] + (1.0 - beta_one) * grad
        moment_new[b] = new
        rows.append(jnp.concatenate([grad.astype(BF16), new.astype(BF16)], axis=0))
    turned = [jnp.dot(rows[b], left[b], preferred_element_type=F32) for b in range(2)]
    pieces = [
        lane_tiles_to_rows(turned[b][16 * x + 8 * half : 16 * x + 8 * half + 8])
        for half in range(2)
        for b in range(2)
        for x in range(2)
    ]
    message[...] = to_messages(pieces)


def step_kernel(arrived, second, right, right_turned, second_new, message):
    turned = from_messages(arrived[...], 64)[:64].astype(BF16)
    ratios = []
    for b in range(2):
        rotated = jnp.dot(turned[32 * b : 32 * b + 32], right[b], preferred_element_type=F32)
        grad, moment = rotated[:16], rotated[16:]
        new = beta_two * second[b] + (1.0 - beta_two) * grad * grad
        second_new[b] = new
        ratio = (moment / bias_one / (jnp.sqrt(new / bias_two) + epsilon)).astype(BF16)
        ratios.append(ratio)
    returned = [jnp.dot(ratios[b], right_turned[b], preferred_element_type=F32) for b in range(2)]
    pieces = [
        lane_tiles_to_rows(returned[b][8 * half : 8 * half + 8])
        for half in range(2)
        for b in range(2)
    ]
    message[...] = to_messages(pieces + [jnp.zeros((64, 128), F32)] * 4)


def back_kernel(
    scale, arrived, left, moment_new, second_new, update, moment_out, second_out, fresh, sems
):
    writes = [
        pltpu.make_async_copy(moment_new, moment_out, sems.at[2]),
        pltpu.make_async_copy(second_new, second_out, sems.at[3]),
    ]
    for write in writes:
        write.start()
    returned = from_messages(arrived[...], 32)[:32].astype(BF16)
    for b in range(2):
        step = jnp.dot(returned[16 * b : 16 * b + 16], left[b], preferred_element_type=F32)
        fresh[b] = scale[b][:, :1] * step
        writes.append(pltpu.make_async_copy(fresh.at[b], update.at[b], sems.at[b]))
        writes[-1].start()
    for write in writes:
        write.wait()


def split_kernel(core, side, parts, away, kept, sems):
    for index in range(2):

        @pl.when(core[0] == index)
        def _():
            if index == 0:
                sources = parts.at[:, :, 1 - side[0]], parts.at[:, :, side[0]]
            else:
                sources = parts.at[:, 1 - side[0]], parts.at[:, side[0]]
            copies = [
                pltpu.make_async_copy(source, out, sems.at[h])
                for h, (source, out) in enumerate(zip(sources, (away, kept)))
            ]
            for copy in copies:
                copy.start()
            for copy in copies:
                copy.wait()


def hold_kernel(left, right, left_held, right_held, right_turned, left_turned, sems):
    copies = [
        pltpu.make_async_copy(left, left_held, sems.at[0]),
        pltpu.make_async_copy(right, right_held, sems.at[1]),
    ]
    for copy in copies:
        copy.start()
    for b in range(2):
        left_turned[b] = left[b].T
        right_turned[b] = right[b].T
    for copy in copies:
        copy.wait()


def strips():
    return jax.ShapeDtypeStruct((2, 16, 1024), F32)


def messages():
    return jax.ShapeDtypeStruct((512, 128), BF16)


def cost(products, size):
    return pl.CostEstimate(flops=2 * products * 1024 * 1024, bytes_accessed=size, transcendentals=0)


FRESH = [pltpu.VMEM((2, 16, 1024), F32), pltpu.SemaphoreType.DMA((4,))]
ANY = pl.BlockSpec(memory_space=pl.ANY)


def split(core, side, parts):
    half = jax.ShapeDtypeStruct((4, 2, 2, 16, 1024), BF16)
    return pl.pallas_call(
        split_kernel,
        out_shape=(half, half),
        in_specs=[SMEM, SMEM, ANY],
        out_specs=(ANY, ANY),
        scratch_shapes=[pltpu.SemaphoreType.DMA((2,))],
        compiler_params=PARAMS,
        cost_estimate=cost(0, 2 << 20),
        name="split",
    )(core, side, parts)


def hold(left, right):
    basis = jax.ShapeDtypeStruct((2, 1024, 1024), BF16)
    return pl.pallas_call(
        hold_kernel,
        out_shape=(basis, basis, basis, basis),
        in_specs=[VMEM, VMEM],
        out_specs=(ANY, ANY, VMEM, VMEM),
        scratch_shapes=[pltpu.SemaphoreType.DMA((2,))],
        compiler_params=PARAMS,
        cost_estimate=cost(0, 24 << 20),
        name="hold",
    )(left, right)


def turn(shares, momentum, left):
    return pl.pallas_call(
        turn_kernel,
        out_shape=(strips(), messages()),
        in_specs=[VMEM] * 3,
        out_specs=(VMEM, VMEM),
        compiler_params=PARAMS,
        cost_estimate=cost(64, 5 << 20),
        name="turn",
    )(shares, momentum, left)


def step(arrived, second, right, right_turned):
    return pl.pallas_call(
        step_kernel,
        out_shape=(strips(), messages()),
        in_specs=[VMEM] * 4,
        out_specs=(VMEM, VMEM),
        compiler_params=PARAMS,
        cost_estimate=cost(96, 5 << 20),
        name="step",
    )(arrived, second, right, right_turned)


def back(scale, arrived, left, moment_new, second_new):
    return pl.pallas_call(
        back_kernel,
        out_shape=(strips(), strips(), strips()),
        in_specs=[VMEM] * 5,
        out_specs=(ANY, ANY, ANY),
        scratch_shapes=FRESH,
        compiler_params=PARAMS,
        cost_estimate=cost(32, 5 << 20),
        name="back",
    )(scale, arrived, left, moment_new, second_new)


def trade(message):
    return lax.all_to_all(message, MP, split_axis=0, concat_axis=0, tiled=True)


def near_pairs():
    place = {(zl, xl, c): 4 * zl + 2 * xl + c for zl in (0, 1) for xl in (0, 1) for c in (0, 1)}
    return [
        (here, place[(zl, 1 - xl, c)] if c == 0 else place[(1 - zl, xl, c)])
        for (zl, xl, c), here in place.items()
    ]


def sum_groups():
    def place(zh, zl, xl, c):
        return 8 * zh + 4 * zl + 2 * xl + c

    along_z = [[place(zh, zl, xl, 0) for zh in range(4) for zl in (0, 1)] for xl in (0, 1)]
    along_x = [[place(zh, zl, xl, 1) for zh in range(4) for xl in (0, 1)] for zl in (0, 1)]
    return along_z + along_x


def local(grad_parts, momentum, second_moment, left_basis, right_basis, lr_scale):
    parts = grad_parts[0].reshape(4, 2, 2, 2, 16, 1024)
    core = lax.axis_index("c")
    side = jnp.where(core == 0, lax.axis_index("xl"), lax.axis_index("zl")).reshape(1)
    core = core.reshape(1)
    away, kept = split(core, side, parts)
    came = lax.ppermute(away, NEAR, near_pairs())
    scale_rows = jnp.broadcast_to(lr_scale[:, None, None], (2, 16, 128))
    held = hold(left_basis, right_basis)
    kept, scale_rows, held = lax.optimization_barrier((kept, scale_rows, held))
    left, right, right_turned, left_turned = held
    pair = (kept.astype(F32) + came.astype(F32)).astype(BF16).reshape(8, 2, 16, 1024)
    shares = lax.all_to_all(
        pair, GROUP, split_axis=0, concat_axis=0, axis_index_groups=sum_groups(), tiled=True
    )
    moment_new, message = turn(shares, momentum, left)
    second_new, message = step(trade(message), second_moment, right, right_turned)
    return back(scale_rows, trade(message), left_turned, moment_new, second_new)


def solution(mesh):
    fine = Mesh(mesh.devices.reshape(4, 2, 2, 8, 4, 2), DP + MP)
    in_specs = (
        P(DP, None, MP, None),
        P(DP, MP, None),
        P(DP, MP, None),
        P(DP, None, None),
        P(DP, None, None),
        P(DP),
    )
    out_specs = (P(DP, MP, None), P(DP, MP, None), P(DP, MP, None))
    return jax.shard_map(local, mesh=fine, in_specs=in_specs, out_specs=out_specs, check_vma=False)
```

```python
import jax
import jax.numpy as jnp
from jax import lax
from jax.experimental import pallas as pl
from jax.experimental.pallas import tpu as pltpu
from jax.sharding import Mesh, PartitionSpec as P

beta_one = 0.95
beta_two = 0.95
epsilon = 1e-08
bias_one = 1.0 - 0.95**10
bias_two = 1.0 - 0.95**10

MP = ("y", "xh", "c")
DP = ("zh", "zl", "xl")
NEAR = ("zl", "xl", "c")
GROUP = DP + ("c",)
F32 = jnp.float32
BF16 = jnp.bfloat16
VMEM = pl.BlockSpec(memory_space=pltpu.VMEM)
SMEM = pl.BlockSpec(memory_space=pltpu.SMEM)
PARAMS = pltpu.CompilerParams(vmem_limit_bytes=24 * 1024 * 1024)


def swap_groups(pieces):
    lane = lax.broadcasted_iota(jnp.int32, (64, 128), 1)
    pieces = list(pieces)
    for bit in (1, 2, 4):
        low = (lane // (16 * bit)) % 2 == 0
        for first in range(8):
            if first & bit:
                continue
            a, b = pieces[first], pieces[first | bit]
            pieces[first] = jnp.where(low, a, pltpu.roll(b, 16 * bit, 1))
            pieces[first | bit] = jnp.where(low, pltpu.roll(a, 128 - 16 * bit, 1), b)
    return pieces


def lane_tiles_to_rows(eight):
    return jnp.concatenate([eight[:, 128 * t : 128 * t + 128] for t in range(8)], axis=0)


def to_messages(pieces):
    swapped = [piece.reshape(8, 8, 128) for piece in swap_groups(pieces)]
    return jnp.stack(swapped, axis=1).reshape(512, 128).astype(BF16)


def from_messages(arrived, shift):
    wide = arrived.astype(F32)
    later = pltpu.roll(wide, 128 - shift, 1)
    rows = jnp.stack([wide.reshape(64, 8, 128), later.reshape(64, 8, 128)], axis=1)
    return rows.reshape(1024, 128).T


def turn_kernel(shares, moment, left, moment_new, message):
    rows = []
    for b in range(2):
        grad = shares[0, b].astype(F32)
        for r in range(1, 8):
            grad = grad + shares[r, b].astype(F32)
        new = beta_one * moment[b] + (1.0 - beta_one) * grad
        moment_new[b] = new
        rows.append(jnp.concatenate([grad.astype(BF16), new.astype(BF16)], axis=0))
    turned = [jnp.dot(rows[b], left[b], preferred_element_type=F32) for b in range(2)]
    pieces = [
        lane_tiles_to_rows(turned[b][16 * x + 8 * half : 16 * x + 8 * half + 8])
        for half in range(2)
        for b in range(2)
        for x in range(2)
    ]
    message[...] = to_messages(pieces)


def step_kernel(arrived, second, right, right_turned, second_new, message):
    turned = from_messages(arrived[...], 64)[:64].astype(BF16)
    ratios = []
    for b in range(2):
        rotated = jnp.dot(turned[32 * b : 32 * b + 32], right[b], preferred_element_type=F32)
        grad, moment = rotated[:16], rotated[16:]
        new = beta_two * second[b] + (1.0 - beta_two) * grad * grad
        second_new[b] = new
        ratio = (moment / bias_one / (jnp.sqrt(new / bias_two) + epsilon)).astype(BF16)
        ratios.append(ratio)
    returned = [jnp.dot(ratios[b], right_turned[b], preferred_element_type=F32) for b in range(2)]
    pieces = [
        lane_tiles_to_rows(returned[b][8 * half : 8 * half + 8])
        for half in range(2)
        for b in range(2)
    ]
    message[...] = to_messages(pieces + [jnp.zeros((64, 128), F32)] * 4)


def back_kernel(
    scale, arrived, left, moment_new, second_new, update, moment_out, second_out, fresh, sems
):
    writes = [
        pltpu.make_async_copy(moment_new, moment_out, sems.at[2]),
        pltpu.make_async_copy(second_new, second_out, sems.at[3]),
    ]
    for write in writes:
        write.start()
    returned = from_messages(arrived[...], 32)[:32].astype(BF16)
    for b in range(2):
        step = jnp.dot(returned[16 * b : 16 * b + 16], left[b], preferred_element_type=F32)
        fresh[b] = scale[b][:, :1] * step
        writes.append(pltpu.make_async_copy(fresh.at[b], update.at[b], sems.at[b]))
        writes[-1].start()
    for write in writes:
        write.wait()


def split_kernel(core, side, parts, away, kept, sems):
    for index in range(2):

        @pl.when(core[0] == index)
        def _():
            if index == 1:
                sources = parts.at[:, :, 1 - side[0]], parts.at[:, :, side[0]]
            else:
                sources = parts.at[:, 1 - side[0]], parts.at[:, side[0]]
            copies = [
                pltpu.make_async_copy(source, out, sems.at[h])
                for h, (source, out) in enumerate(zip(sources, (away, kept)))
            ]
            for copy in copies:
                copy.start()
            for copy in copies:
                copy.wait()


def hold_kernel(left, right, left_held, right_held, right_turned, left_turned, sems):
    copies = [
        pltpu.make_async_copy(left, left_held, sems.at[0]),
        pltpu.make_async_copy(right, right_held, sems.at[1]),
    ]
    for copy in copies:
        copy.start()
    for b in range(2):
        left_turned[b] = left[b].T
        right_turned[b] = right[b].T
    for copy in copies:
        copy.wait()


def strips():
    return jax.ShapeDtypeStruct((2, 16, 1024), F32)


def messages():
    return jax.ShapeDtypeStruct((512, 128), BF16)


def cost(products, size):
    return pl.CostEstimate(flops=2 * products * 1024 * 1024, bytes_accessed=size, transcendentals=0)


FRESH = [pltpu.VMEM((2, 16, 1024), F32), pltpu.SemaphoreType.DMA((4,))]
ANY = pl.BlockSpec(memory_space=pl.ANY)


def split(core, side, parts):
    half = jax.ShapeDtypeStruct((4, 2, 2, 16, 1024), BF16)
    return pl.pallas_call(
        split_kernel,
        out_shape=(half, half),
        in_specs=[SMEM, SMEM, ANY],
        out_specs=(ANY, ANY),
        scratch_shapes=[pltpu.SemaphoreType.DMA((2,))],
        compiler_params=PARAMS,
        cost_estimate=cost(0, 2 << 20),
        name="split",
    )(core, side, parts)


def hold(left, right):
    basis = jax.ShapeDtypeStruct((2, 1024, 1024), BF16)
    return pl.pallas_call(
        hold_kernel,
        out_shape=(basis, basis, basis, basis),
        in_specs=[VMEM, VMEM],
        out_specs=(ANY, ANY, VMEM, VMEM),
        scratch_shapes=[pltpu.SemaphoreType.DMA((2,))],
        compiler_params=PARAMS,
        cost_estimate=cost(0, 24 << 20),
        name="hold",
    )(left, right)


def turn(shares, momentum, left):
    return pl.pallas_call(
        turn_kernel,
        out_shape=(strips(), messages()),
        in_specs=[VMEM] * 3,
        out_specs=(VMEM, VMEM),
        compiler_params=PARAMS,
        cost_estimate=cost(64, 5 << 20),
        name="turn",
    )(shares, momentum, left)


def step(arrived, second, right, right_turned):
    return pl.pallas_call(
        step_kernel,
        out_shape=(strips(), messages()),
        in_specs=[VMEM] * 4,
        out_specs=(VMEM, VMEM),
        compiler_params=PARAMS,
        cost_estimate=cost(96, 5 << 20),
        name="step",
    )(arrived, second, right, right_turned)


def back(scale, arrived, left, moment_new, second_new):
    return pl.pallas_call(
        back_kernel,
        out_shape=(strips(), strips(), strips()),
        in_specs=[VMEM] * 5,
        out_specs=(ANY, ANY, ANY),
        scratch_shapes=FRESH,
        compiler_params=PARAMS,
        cost_estimate=cost(32, 5 << 20),
        name="back",
    )(scale, arrived, left, moment_new, second_new)


def trade(message):
    return lax.all_to_all(message, MP, split_axis=0, concat_axis=0, tiled=True)


def near_pairs():
    place = {(zl, xl, c): 4 * zl + 2 * xl + c for zl in (0, 1) for xl in (0, 1) for c in (0, 1)}
    return [
        (here, place[(zl, 1 - xl, c)] if c == 1 else place[(1 - zl, xl, c)])
        for (zl, xl, c), here in place.items()
    ]


def sum_groups():
    def place(zh, zl, xl, c):
        return 8 * zh + 4 * zl + 2 * xl + c

    along_z = [[place(zh, zl, xl, 1) for zh in range(4) for zl in (0, 1)] for xl in (0, 1)]
    along_x = [[place(zh, zl, xl, 0) for zh in range(4) for xl in (0, 1)] for zl in (0, 1)]
    return along_z + along_x


def local(grad_parts, momentum, second_moment, left_basis, right_basis, lr_scale):
    parts = grad_parts[0].reshape(4, 2, 2, 2, 16, 1024)
    core = lax.axis_index("c")
    side = jnp.where(core == 1, lax.axis_index("xl"), lax.axis_index("zl")).reshape(1)
    core = core.reshape(1)
    away, kept = split(core, side, parts)
    came = lax.ppermute(away, NEAR, near_pairs())
    scale_rows = jnp.broadcast_to(lr_scale[:, None, None], (2, 16, 128))
    held = hold(left_basis, right_basis)
    kept, scale_rows, held = lax.optimization_barrier((kept, scale_rows, held))
    left, right, right_turned, left_turned = held
    pair = (kept.astype(F32) + came.astype(F32)).astype(BF16).reshape(8, 2, 16, 1024)
    shares = lax.all_to_all(
        pair, GROUP, split_axis=0, concat_axis=0, axis_index_groups=sum_groups(), tiled=True
    )
    moment_new, message = turn(shares, momentum, left)
    second_new, message = step(trade(message), second_moment, right, right_turned)
    return back(scale_rows, trade(message), left_turned, moment_new, second_new)


def solution(mesh):
    fine = Mesh(mesh.devices.reshape(4, 2, 2, 8, 4, 2), DP + MP)
    in_specs = (
        P(DP, None, MP, None),
        P(DP, MP, None),
        P(DP, MP, None),
        P(DP, None, None),
        P(DP, None, None),
        P(DP),
    )
    out_specs = (P(DP, MP, None), P(DP, MP, None), P(DP, MP, None))
    return jax.shard_map(local, mesh=fine, in_specs=in_specs, out_specs=out_specs, check_vma=False)
```

```python
import jax
import jax.numpy as jnp
from jax import lax
from jax.experimental import pallas as pl
from jax.experimental.pallas import tpu as pltpu
from jax.sharding import Mesh, PartitionSpec as P

beta_one = 0.95
beta_two = 0.95
epsilon = 1e-08
bias_one = 1.0 - 0.95**10
bias_two = 1.0 - 0.95**10

MP = ("y", "xh", "c")
DP = ("zh", "zl", "xl")
NEAR = ("zl", "xl", "c")
GROUP = DP + ("c",)
F32 = jnp.float32
BF16 = jnp.bfloat16
VMEM = pl.BlockSpec(memory_space=pltpu.VMEM)
SMEM = pl.BlockSpec(memory_space=pltpu.SMEM)
PARAMS = pltpu.CompilerParams(vmem_limit_bytes=24 * 1024 * 1024)


def swap_groups(pieces):
    lane = lax.broadcasted_iota(jnp.int32, (64, 128), 1)
    pieces = list(pieces)
    for bit in (1, 2, 4):
        low = (lane // (16 * bit)) % 2 == 0
        for first in range(8):
            if first & bit:
                continue
            a, b = pieces[first], pieces[first | bit]
            pieces[first] = jnp.where(low, a, pltpu.roll(b, 16 * bit, 1))
            pieces[first | bit] = jnp.where(low, pltpu.roll(a, 128 - 16 * bit, 1), b)
    return pieces


def lane_tiles_to_rows(eight):
    return jnp.concatenate([eight[:, 128 * t : 128 * t + 128] for t in range(8)], axis=0)


def to_messages(pieces):
    swapped = [piece.reshape(8, 8, 128) for piece in swap_groups(pieces)]
    return jnp.stack(swapped, axis=1).reshape(512, 128).astype(BF16)


def from_messages(arrived, shift):
    wide = arrived.astype(F32)
    later = pltpu.roll(wide, 128 - shift, 1)
    rows = jnp.stack([wide.reshape(64, 8, 128), later.reshape(64, 8, 128)], axis=1)
    return rows.reshape(1024, 128).T


def turn_kernel(shares, moment, left, moment_new, message):
    rows = []
    for b in range(2):
        grad = shares[0, b].astype(F32)
        for r in range(1, 8):
            grad = grad + shares[r, b].astype(F32)
        new = beta_one * moment[b] + (1.0 - beta_one) * grad
        moment_new[b] = new
        rows.append(jnp.concatenate([grad.astype(BF16), new.astype(BF16)], axis=0))
    turned = [jnp.dot(rows[b], left[b], preferred_element_type=F32) for b in range(2)]
    pieces = [
        lane_tiles_to_rows(turned[b][16 * x + 8 * half : 16 * x + 8 * half + 8])
        for half in range(2)
        for b in range(2)
        for x in range(2)
    ]
    message[...] = to_messages(pieces)


def step_kernel(arrived, second, right, right_turned, second_new, message):
    turned = from_messages(arrived[...], 64)[:64].astype(BF16)
    ratios = []
    for b in range(2):
        rotated = jnp.dot(turned[32 * b : 32 * b + 32], right[b], preferred_element_type=F32)
        grad, moment = rotated[:16], rotated[16:]
        new = beta_two * second[b] + (1.0 - beta_two) * grad * grad
        second_new[b] = new
        ratio = (moment / bias_one / (jnp.sqrt(new / bias_two) + epsilon)).astype(BF16)
        ratios.append(ratio)
    returned = [jnp.dot(ratios[b], right_turned[b], preferred_element_type=F32) for b in range(2)]
    pieces = [
        lane_tiles_to_rows(returned[b][8 * half : 8 * half + 8])
        for half in range(2)
        for b in range(2)
    ]
    message[...] = to_messages(pieces + [jnp.zeros((64, 128), F32)] * 4)


def back_kernel(
    scale, arrived, left, moment_new, second_new, update, moment_out, second_out, fresh, sems
):
    writes = [
        pltpu.make_async_copy(moment_new, moment_out, sems.at[2]),
        pltpu.make_async_copy(second_new, second_out, sems.at[3]),
    ]
    for write in writes:
        write.start()
    returned = from_messages(arrived[...], 32)[:32].astype(BF16)
    for b in range(2):
        step = jnp.dot(returned[16 * b : 16 * b + 16], left[b], preferred_element_type=F32)
        fresh[b] = scale[b][:, :1] * step
        writes.append(pltpu.make_async_copy(fresh.at[b], update.at[b], sems.at[b]))
        writes[-1].start()
    for write in writes:
        write.wait()


def split_kernel(core, side, parts, away, kept, sems):
    mine, other = side[0], 1 - side[0]
    low, high = pl.ds(0, 2), pl.ds(2, 2)
    plans = (
        (
            (parts.at[low, other], away.at[low]),
            (parts.at[high, mine], away.at[high]),
            (parts.at[low, mine], kept.at[low]),
            (parts.at[high, other], kept.at[high]),
        ),
        ((parts.at[:, :, other], away), (parts.at[:, :, mine], kept)),
    )
    for index, plan in enumerate(plans):

        @pl.when(core[0] == index)
        def _():
            copies = [
                pltpu.make_async_copy(source, out, sems.at[h])
                for h, (source, out) in enumerate(plan)
            ]
            for copy in copies:
                copy.start()
            for copy in copies:
                copy.wait()


def hold_kernel(left, right, left_held, right_held, right_turned, left_turned, sems):
    copies = [
        pltpu.make_async_copy(left, left_held, sems.at[0]),
        pltpu.make_async_copy(right, right_held, sems.at[1]),
    ]
    for copy in copies:
        copy.start()
    for b in range(2):
        left_turned[b] = left[b].T
        right_turned[b] = right[b].T
    for copy in copies:
        copy.wait()


def strips():
    return jax.ShapeDtypeStruct((2, 16, 1024), F32)


def messages():
    return jax.ShapeDtypeStruct((512, 128), BF16)


def cost(products, size):
    return pl.CostEstimate(flops=2 * products * 1024 * 1024, bytes_accessed=size, transcendentals=0)


FRESH = [pltpu.VMEM((2, 16, 1024), F32), pltpu.SemaphoreType.DMA((4,))]
ANY = pl.BlockSpec(memory_space=pl.ANY)


def split(core, side, parts):
    half = jax.ShapeDtypeStruct((4, 2, 2, 16, 1024), BF16)
    return pl.pallas_call(
        split_kernel,
        out_shape=(half, half),
        in_specs=[SMEM, SMEM, ANY],
        out_specs=(ANY, ANY),
        scratch_shapes=[pltpu.SemaphoreType.DMA((4,))],
        compiler_params=PARAMS,
        cost_estimate=cost(0, 2 << 20),
        name="split",
    )(core, side, parts)


def hold(left, right):
    basis = jax.ShapeDtypeStruct((2, 1024, 1024), BF16)
    return pl.pallas_call(
        hold_kernel,
        out_shape=(basis, basis, basis, basis),
        in_specs=[VMEM, VMEM],
        out_specs=(ANY, ANY, VMEM, VMEM),
        scratch_shapes=[pltpu.SemaphoreType.DMA((2,))],
        compiler_params=PARAMS,
        cost_estimate=cost(0, 24 << 20),
        name="hold",
    )(left, right)


def turn(shares, momentum, left):
    return pl.pallas_call(
        turn_kernel,
        out_shape=(strips(), messages()),
        in_specs=[VMEM] * 3,
        out_specs=(VMEM, VMEM),
        compiler_params=PARAMS,
        cost_estimate=cost(64, 5 << 20),
        name="turn",
    )(shares, momentum, left)


def step(arrived, second, right, right_turned):
    return pl.pallas_call(
        step_kernel,
        out_shape=(strips(), messages()),
        in_specs=[VMEM] * 4,
        out_specs=(VMEM, VMEM),
        compiler_params=PARAMS,
        cost_estimate=cost(96, 5 << 20),
        name="step",
    )(arrived, second, right, right_turned)


def back(scale, arrived, left, moment_new, second_new):
    return pl.pallas_call(
        back_kernel,
        out_shape=(strips(), strips(), strips()),
        in_specs=[VMEM] * 5,
        out_specs=(ANY, ANY, ANY),
        scratch_shapes=FRESH,
        compiler_params=PARAMS,
        cost_estimate=cost(32, 5 << 20),
        name="back",
    )(scale, arrived, left, moment_new, second_new)


def trade(message):
    return lax.all_to_all(message, MP, split_axis=0, concat_axis=0, tiled=True)


def near_pairs():
    place = {(zl, xl, c): 4 * zl + 2 * xl + c for zl in (0, 1) for xl in (0, 1) for c in (0, 1)}
    return [
        (here, place[(zl, 1 - xl, c)] if c == 1 else place[(1 - zl, xl, c)])
        for (zl, xl, c), here in place.items()
    ]


def z_set(zh, zl):
    return (zl + zh // 2) % 2


def sum_groups():
    def place(zh, zl, xl, c):
        return 8 * zh + 4 * zl + 2 * xl + c

    along_z = [[place(zh, zl, xl, 1) for zh in range(4) for zl in (0, 1)] for xl in (0, 1)]
    by_set = [
        [place(zh, z_set(zh, member), xl, 0) for zh in range(4) for xl in (0, 1)]
        for member in (0, 1)
    ]
    return along_z + by_set


def local(grad_parts, momentum, second_moment, left_basis, right_basis, lr_scale):
    parts = grad_parts[0].reshape(4, 2, 2, 2, 16, 1024)
    core = lax.axis_index("c")
    member = z_set(lax.axis_index("zh"), lax.axis_index("zl"))
    side = jnp.where(core == 1, lax.axis_index("xl"), member).reshape(1)
    core = core.reshape(1)
    away, kept = split(core, side, parts)
    came = lax.ppermute(away, NEAR, near_pairs())
    scale_rows = jnp.broadcast_to(lr_scale[:, None, None], (2, 16, 128))
    held = hold(left_basis, right_basis)
    kept, scale_rows, held = lax.optimization_barrier((kept, scale_rows, held))
    left, right, right_turned, left_turned = held
    pair = (kept.astype(F32) + came.astype(F32)).astype(BF16).reshape(8, 2, 16, 1024)
    shares = lax.all_to_all(
        pair, GROUP, split_axis=0, concat_axis=0, axis_index_groups=sum_groups(), tiled=True
    )
    moment_new, message = turn(shares, momentum, left)
    second_new, message = step(trade(message), second_moment, right, right_turned)
    return back(scale_rows, trade(message), left_turned, moment_new, second_new)


def solution(mesh):
    fine = Mesh(mesh.devices.reshape(4, 2, 2, 8, 4, 2), DP + MP)
    in_specs = (
        P(DP, None, MP, None),
        P(DP, MP, None),
        P(DP, MP, None),
        P(DP, None, None),
        P(DP, None, None),
        P(DP),
    )
    out_specs = (P(DP, MP, None), P(DP, MP, None), P(DP, MP, None))
    return jax.shard_map(local, mesh=fine, in_specs=in_specs, out_specs=out_specs, check_vma=False)
```

```python
import jax
import jax.numpy as jnp
from jax import lax
from jax.experimental import pallas as pl
from jax.experimental.pallas import tpu as pltpu
from jax.sharding import Mesh, PartitionSpec as P

beta_one = 0.95
beta_two = 0.95
epsilon = 1e-08
bias_one = 1.0 - 0.95**10
bias_two = 1.0 - 0.95**10

MP = ("y", "xh", "c")
DP = ("zh", "zl", "xl")
GROUP = DP + ("c",)
F32 = jnp.float32
BF16 = jnp.bfloat16
VMEM = pl.BlockSpec(memory_space=pltpu.VMEM)
SMEM = pl.BlockSpec(memory_space=pltpu.SMEM)
PARAMS = pltpu.CompilerParams(vmem_limit_bytes=24 * 1024 * 1024)


def swap_groups(pieces):
    lane = lax.broadcasted_iota(jnp.int32, (64, 128), 1)
    pieces = list(pieces)
    for bit in (1, 2, 4):
        low = (lane // (16 * bit)) % 2 == 0
        for first in range(8):
            if first & bit:
                continue
            a, b = pieces[first], pieces[first | bit]
            pieces[first] = jnp.where(low, a, pltpu.roll(b, 16 * bit, 1))
            pieces[first | bit] = jnp.where(low, pltpu.roll(a, 128 - 16 * bit, 1), b)
    return pieces


def lane_tiles_to_rows(eight):
    return jnp.concatenate([eight[:, 128 * t : 128 * t + 128] for t in range(8)], axis=0)


def to_messages(pieces):
    swapped = [piece.reshape(8, 8, 128) for piece in swap_groups(pieces)]
    return jnp.stack(swapped, axis=1).reshape(512, 128).astype(BF16)


def from_messages(arrived, shift):
    wide = arrived.astype(F32)
    later = pltpu.roll(wide, 128 - shift, 1)
    rows = jnp.stack([wide.reshape(64, 8, 128), later.reshape(64, 8, 128)], axis=1)
    return rows.reshape(1024, 128).T


def turn_kernel(shares, moment, left, moment_new, message):
    rows = []
    for b in range(2):
        grad = shares[0, b].astype(F32)
        for r in range(1, 8):
            grad = grad + shares[r, b].astype(F32)
        new = beta_one * moment[b] + (1.0 - beta_one) * grad
        moment_new[b] = new
        rows.append(jnp.concatenate([grad.astype(BF16), new.astype(BF16)], axis=0))
    turned = [jnp.dot(rows[b], left[b], preferred_element_type=F32) for b in range(2)]
    pieces = [
        lane_tiles_to_rows(turned[b][16 * x + 8 * half : 16 * x + 8 * half + 8])
        for half in range(2)
        for b in range(2)
        for x in range(2)
    ]
    message[...] = to_messages(pieces)


def step_kernel(arrived, second, right, right_turned, second_new, message):
    turned = from_messages(arrived[...], 64)[:64].astype(BF16)
    ratios = []
    for b in range(2):
        rotated = jnp.dot(turned[32 * b : 32 * b + 32], right[b], preferred_element_type=F32)
        grad, moment = rotated[:16], rotated[16:]
        new = beta_two * second[b] + (1.0 - beta_two) * grad * grad
        second_new[b] = new
        ratio = (moment / bias_one / (jnp.sqrt(new / bias_two) + epsilon)).astype(BF16)
        ratios.append(ratio)
    returned = [jnp.dot(ratios[b], right_turned[b], preferred_element_type=F32) for b in range(2)]
    pieces = [
        lane_tiles_to_rows(returned[b][8 * half : 8 * half + 8])
        for half in range(2)
        for b in range(2)
    ]
    message[...] = to_messages(pieces + [jnp.zeros((64, 128), F32)] * 4)


def back_kernel(
    scale, arrived, left, moment_new, second_new, update, moment_out, second_out, fresh, sems
):
    writes = [
        pltpu.make_async_copy(moment_new, moment_out, sems.at[2]),
        pltpu.make_async_copy(second_new, second_out, sems.at[3]),
    ]
    for write in writes:
        write.start()
    returned = from_messages(arrived[...], 32)[:32].astype(BF16)
    for b in range(2):
        step = jnp.dot(returned[16 * b : 16 * b + 16], left[b], preferred_element_type=F32)
        fresh[b] = scale[b][:, :1] * step
        writes.append(pltpu.make_async_copy(fresh.at[b], update.at[b], sems.at[b]))
        writes[-1].start()
    for write in writes:
        write.wait()


def z_set(z):
    return (z % 2 + z // 4) % 2


def z_members(c, member):
    return [z for z in range(8) if z_set((z - c) % 8) == member]


def split_kernel(core, side, parts, away, kept, sems):
    def z_of(member, place):
        first, second = (
            jnp.where(member == 0, z_members(c, 0)[place], z_members(c, 1)[place]) for c in (0, 1)
        )
        return jnp.where(core[0] == 0, first, second)

    copies = []
    for place in range(4):
        for member, out in ((1 - side[0], away), (side[0], kept)):
            copies.append(
                pltpu.make_async_copy(
                    parts.at[z_of(member, place)], out.at[place], sems.at[len(copies)]
                )
            )
    for copy in copies:
        copy.start()
    for copy in copies:
        copy.wait()


def hold_kernel(left, right, left_held, right_held, right_turned, left_turned, sems):
    copies = [
        pltpu.make_async_copy(left, left_held, sems.at[0]),
        pltpu.make_async_copy(right, right_held, sems.at[1]),
    ]
    for copy in copies:
        copy.start()
    for b in range(2):
        left_turned[b] = left[b].T
        right_turned[b] = right[b].T
    for copy in copies:
        copy.wait()


def strips():
    return jax.ShapeDtypeStruct((2, 16, 1024), F32)


def messages():
    return jax.ShapeDtypeStruct((512, 128), BF16)


def cost(products, size):
    return pl.CostEstimate(flops=2 * products * 1024 * 1024, bytes_accessed=size, transcendentals=0)


FRESH = [pltpu.VMEM((2, 16, 1024), F32), pltpu.SemaphoreType.DMA((4,))]
ANY = pl.BlockSpec(memory_space=pl.ANY)


def split(core, side, parts):
    half = jax.ShapeDtypeStruct((4, 2, 2, 16, 1024), BF16)
    return pl.pallas_call(
        split_kernel,
        out_shape=(half, half),
        in_specs=[SMEM, SMEM, ANY],
        out_specs=(ANY, ANY),
        scratch_shapes=[pltpu.SemaphoreType.DMA((8,))],
        compiler_params=PARAMS,
        cost_estimate=cost(0, 2 << 20),
        name="split",
    )(core, side, parts)


def hold(left, right):
    basis = jax.ShapeDtypeStruct((2, 1024, 1024), BF16)
    return pl.pallas_call(
        hold_kernel,
        out_shape=(basis, basis, basis, basis),
        in_specs=[VMEM, VMEM],
        out_specs=(ANY, ANY, VMEM, VMEM),
        scratch_shapes=[pltpu.SemaphoreType.DMA((2,))],
        compiler_params=PARAMS,
        cost_estimate=cost(0, 24 << 20),
        name="hold",
    )(left, right)


def turn(shares, momentum, left):
    return pl.pallas_call(
        turn_kernel,
        out_shape=(strips(), messages()),
        in_specs=[VMEM] * 3,
        out_specs=(VMEM, VMEM),
        compiler_params=PARAMS,
        cost_estimate=cost(64, 5 << 20),
        name="turn",
    )(shares, momentum, left)


def step(arrived, second, right, right_turned):
    return pl.pallas_call(
        step_kernel,
        out_shape=(strips(), messages()),
        in_specs=[VMEM] * 4,
        out_specs=(VMEM, VMEM),
        compiler_params=PARAMS,
        cost_estimate=cost(96, 5 << 20),
        name="step",
    )(arrived, second, right, right_turned)


def back(scale, arrived, left, moment_new, second_new):
    return pl.pallas_call(
        back_kernel,
        out_shape=(strips(), strips(), strips()),
        in_specs=[VMEM] * 5,
        out_specs=(ANY, ANY, ANY),
        scratch_shapes=FRESH,
        compiler_params=PARAMS,
        cost_estimate=cost(32, 5 << 20),
        name="back",
    )(scale, arrived, left, moment_new, second_new)


def trade(message):
    return lax.all_to_all(message, MP, split_axis=0, concat_axis=0, tiled=True)


def place(z, xl, c):
    return 4 * z + 2 * xl + c


def near_pairs():
    return [
        (place(z, xl, c), place((((z - c) % 8 ^ 1) + c) % 8, xl, c))
        for z in range(8)
        for xl in (0, 1)
        for c in (0, 1)
    ]


def sum_groups():
    return [
        [place(z, xl, c) for z in z_members(c, member) for xl in (0, 1)]
        for c in (0, 1)
        for member in (0, 1)
    ]


def local(grad_parts, momentum, second_moment, left_basis, right_basis, lr_scale):
    parts = grad_parts[0].reshape(8, 2, 2, 16, 1024)
    core = lax.axis_index("c")
    z = 2 * lax.axis_index("zh") + lax.axis_index("zl")
    side = z_set((z + 8 - core) % 8).reshape(1)
    core = core.reshape(1)
    away, kept = split(core, side, parts)
    came = lax.ppermute(away, GROUP, near_pairs())
    scale_rows = jnp.broadcast_to(lr_scale[:, None, None], (2, 16, 128))
    held = hold(left_basis, right_basis)
    kept, scale_rows, held = lax.optimization_barrier((kept, scale_rows, held))
    left, right, right_turned, left_turned = held
    pair = (kept.astype(F32) + came.astype(F32)).astype(BF16).reshape(8, 2, 16, 1024)
    shares = lax.all_to_all(
        pair, GROUP, split_axis=0, concat_axis=0, axis_index_groups=sum_groups(), tiled=True
    )
    moment_new, message = turn(shares, momentum, left)
    second_new, message = step(trade(message), second_moment, right, right_turned)
    return back(scale_rows, trade(message), left_turned, moment_new, second_new)


def solution(mesh):
    fine = Mesh(mesh.devices.reshape(4, 2, 2, 8, 4, 2), DP + MP)
    in_specs = (
        P(DP, None, MP, None),
        P(DP, MP, None),
        P(DP, MP, None),
        P(DP, None, None),
        P(DP, None, None),
        P(DP),
    )
    out_specs = (P(DP, MP, None), P(DP, MP, None), P(DP, MP, None))
    return jax.shard_map(local, mesh=fine, in_specs=in_specs, out_specs=out_specs, check_vma=False)
```
